128 devices in a mesh: ex: 16 (over y_lo, x, core), ey: 8 (over y_hi, z).
Axes of the slice: x: 4, y: 4 (y_hi: 2, y_lo: 2; y = y_hi * 2 + y_lo), z: 4, core: 2. Of those that a mesh axis runs over, the one named last changes fastest.
Arguments:
- settings: float32 [512, 16], replicated, may hold values from -1 to 1
- frequencies: float32 [16, 2048], replicated, may hold values from -4 to 4
- phases: float32 [2048], replicated, may hold values from -3.140625 to 3.140625
- noise_var: float32 [128], replicated, may hold values from 0.01 to 0.1
- signal_scale: float32 [128], replicated, may hold values from 0.5 to 2
- cov_factor: bfloat16 [256, 2048, 2048], P(('ex', 'ey')), as said below
- post_mean: bfloat16 [256, 2048, 128], P(('ex', 'ey')), may hold values from -6 to 6
- component_basis: bfloat16 [128, 1048576], P('ey', 'ex'), may hold values from -0.5 to 0.5
- mean_field: float32 [1048576], P(('ex', 'ey')), may hold values from -4 to 4
Outputs:
- carbon: bfloat16 [512, 1048576], P(None, ('ex', 'ey'))
The draws below stay inside these ranges and needn't reach their ends.
Inputs may be any that keep to these rules, and one draw needn't show every extreme that they name: `cov_factor`: entries of expert k's factor lie within 8 / sqrt(log(2049)) of zero.
All inputs are finite; a program needn't handle non-finite values.
Results may differ from the reference program's by a relative error of at most 0.0037.
Values may be sent and summed in bfloat16 or wider, within the bound.
No kernel may reach another device: no remote copies, remote signals or barrier semaphores. Data moves between devices by JAX's collectives and lax.ppermute only.
A program may use at most 128 MiB of HBM per device.

```python
import math
import jax
import jax.numpy as jnp
from jax import lax

PARAMS = 16
FEAT = 2048
COMP = 128
SETTINGS = 512
EXPERTS = 256
CELLS = 1048576


def draw_cov_factor(key, part):
    key_gain = jax.random.fold_in(key, 11)
    key_noise = jax.random.fold_in(key, 23)
    key_column = jax.random.fold_in(key, 37)
    gains = jnp.exp(jax.random.uniform(key_gain, (EXPERTS, 1, 1), jnp.float32, math.log(0.2), math.log(2.0)))
    draws_column = jax.random.uniform(key_column, (EXPERTS, 1, FEAT), jnp.float32, 0.0, 1.0)
    column_weight = 1.0 / (1.0 + draws_column * FEAT)
    column_scale = jnp.sqrt(column_weight / math.log(1.0 + FEAT))
    values = jax.random.truncated_normal(key_noise, -4.0, 4.0, (EXPERTS, FEAT, FEAT), jnp.float32)
    return (values * gains * column_scale).astype(jnp.bfloat16)


def level_of(stream_key, extent, cuts, least, top_value):
    loudness, own = 1.0, jax.random.fold_in(stream_key, 6)
    for dim, parts in cuts:
        draws = jnp.exp(jax.random.uniform(jax.random.fold_in(own, dim), (parts,), jnp.float32, least / len(cuts), top_value / len(cuts)))
        loudness = loudness * jnp.repeat(draws, extent[dim] // parts).reshape([-1 if axis == dim else 1 for axis in range(len(extent))])
    return loudness


def gaussian(own_key, dims, width, most, cuts=(), dtype=jnp.bfloat16):
    array = width * jax.random.normal(own_key, dims, jnp.float32)
    if cuts:
        array = array * level_of(own_key, dims, cuts, -0.22, 0.18)
    return jnp.clip(array, -most, most).astype(dtype)


def setup_inputs(seed: int = 0) -> dict:
    arg_keys = jax.random.split(jax.random.key(seed), 10)
    settings = jnp.clip(jax.random.uniform(arg_keys[0], (SETTINGS, PARAMS), jnp.float32, -1.0, 1.0), -1.0, 1.0)
    frequencies = gaussian(arg_keys[1], (PARAMS, FEAT), 1.0, 4.0, (), jnp.float32)
    phases = jnp.clip(jax.random.uniform(arg_keys[2], (FEAT,), jnp.float32, -3.140625, 3.140625), -3.140625, 3.140625)
    noise_var = jnp.clip(jnp.exp(jax.random.uniform(arg_keys[3], (COMP,), jnp.float32, math.log(0.01), math.log(0.1))), 0.01, 0.1)
    signal_scale = jnp.clip(jnp.exp(jax.random.uniform(arg_keys[4], (COMP,), jnp.float32, math.log(0.5), math.log(2.0))), 0.5, 2.0)
    cov_factor = draw_cov_factor(jax.random.fold_in(arg_keys[9], 71), 0)
    post_mean = gaussian(arg_keys[6], (EXPERTS, FEAT, COMP), 1.0, 6.0, ((0, 128),))
    component_basis = gaussian(arg_keys[7], (COMP, CELLS), COMP ** -0.5, 0.5, ((0, 8), (1, 16)))
    mean_field = gaussian(arg_keys[8], (CELLS,), 0.25, 4.0, ((0, 128),), jnp.float32)
    return {"settings": settings, "frequencies": frequencies, "phases": phases, "noise_var": noise_var, "signal_scale": signal_scale, "cov_factor": cov_factor, "post_mean": post_mean, "component_basis": component_basis, "mean_field": mean_field}


def feature_map(settings, frequencies, phases):
    argument = jnp.dot(settings, frequencies, precision=lax.Precision.HIGHEST, preferred_element_type=jnp.float32)
    return (jnp.sqrt(2.0 / FEAT) * jnp.cos(argument + phases[None, :])).astype(jnp.bfloat16)

def reference(settings, frequencies, phases, noise_var, signal_scale, cov_factor, post_mean, component_basis, mean_field):
    feature_rows = feature_map(settings, frequencies, phases)
    feature_float = feature_rows.astype(jnp.float32)
    feature_norm = lax.optimization_barrier(jnp.sum(feature_float * feature_float, axis=1))
    prior_var = noise_var[None, :] + signal_scale[None, :] * feature_norm[:, None]

    def accumulate(running, operands):
        numerator, precision = running
        factor, expert_means = operands
        projected = jnp.dot(feature_rows, factor, preferred_element_type=jnp.float32)
        spread = lax.optimization_barrier(jnp.sum(projected * projected, axis=1))
        expert_mean = jnp.dot(feature_rows, expert_means, preferred_element_type=jnp.float32)
        variance = noise_var[None, :] + signal_scale[None, :] * spread[:, None]
        robust_weight = jnp.maximum(0.5 * (jnp.log(prior_var) - jnp.log(variance)), 0.0)
        numerator = numerator + robust_weight / variance * expert_mean
        precision = precision + robust_weight * (1.0 / variance - 1.0 / prior_var)
        return ((numerator, precision), None)
    zeros_init = jnp.zeros((SETTINGS, COMP), jnp.float32)
    (numerator, precision), _ = lax.scan(accumulate, (zeros_init, zeros_init), (cov_factor, post_mean))
    weights = (numerator / (precision + 1.0 / prior_var)).astype(jnp.bfloat16)
    stock = jnp.dot(weights, component_basis, preferred_element_type=jnp.float32) + mean_field[None, :]
    return stock.astype(jnp.bfloat16)
```

```python
import functools
import math

import jax
import jax.numpy as jnp
import numpy as np
from jax import lax
from jax.experimental import pallas as pl
from jax.experimental.pallas import tpu as pltpu
from jax.sharding import PartitionSpec as P

AXES = ("ex", "ey")
COLUMNS = 512
ROWS = 32
LANES = 128


def sine_coefficients(terms):
    nodes = 64
    square = (1 / 16) * (0.5 + 0.5 * np.cos((2 * np.arange(nodes) + 1) * np.pi / (2 * nodes)))
    w = np.sqrt(square)
    powers = np.stack([square**i for i in range(terms)], 1) * w[:, None]
    fit, *_ = np.linalg.lstsq(powers, np.sin(2 * np.pi * w), rcond=None)
    return [float(c) for c in fit]


def split(values):
    high = values.astype(jnp.bfloat16)
    rest = values - high.astype(jnp.float32)
    middle = rest.astype(jnp.bfloat16)
    low = (rest - middle.astype(jnp.float32)).astype(jnp.bfloat16)
    return high, middle, low


def experts_kernel(
    devices,
    settings_hbm,
    frequencies_hbm,
    phases_hbm,
    noise_hbm,
    scale_hbm,
    factor_hbm,
    mean_hbm,
    out_ref,
    settings,
    frequencies,
    phases,
    noise,
    scale,
    factor,
    means,
    phi,
    argument,
    squares,
    small_sems,
    sems,
):
    experts, feats, _ = factor.shape
    rows = phi.shape[0]
    chunks = feats // COLUMNS
    small = [
        pltpu.make_async_copy(source, target, small_sems.at[i])
        for i, (source, target) in enumerate(
            (
                (settings_hbm, settings),
                (frequencies_hbm, frequencies),
                (phases_hbm, phases),
                (noise_hbm, noise),
                (scale_hbm, scale),
                (mean_hbm, means),
            )
        )
    ]
    large = [
        pltpu.make_async_copy(
            factor_hbm.at[e, :, pl.ds(n * COLUMNS, COLUMNS)],
            factor.at[e, :, pl.ds(n * COLUMNS, COLUMNS)],
            sems.at[e * chunks + n],
        )
        for e in range(experts)
        for n in range(chunks)
    ]
    for copy in small[:5] + large + small[5:]:
        copy.start()
    for copy in small[:5]:
        copy.wait()

    turn = 1.0 / (2.0 * math.pi)
    a0, a1, a2 = split(settings[...])
    b0, b1, b2 = split(frequencies[...] * turn)
    argument[...] = lax.dot_general(
        jnp.concatenate([a0, a0, a1, a1, a0, a2], 0),
        jnp.concatenate([b0, b1, b0, b1, b2, b0], 0),
        (((0,), (0,)), ((), ())),
        preferred_element_type=jnp.float32,
    )
    amplitude = math.sqrt(2.0 / feats)
    coefficients = [c * amplitude for c in sine_coefficients(5)]

    def feature_rows(r, carry):
        block = pl.ds(pl.multiple_of(r * ROWS, ROWS), ROWS)
        total = jnp.zeros((ROWS, LANES), jnp.float32)
        for c in range(feats // 512):
            span = slice(c * 512, (c + 1) * 512)
            turns = argument[block, span] + phases[:, span] * turn
            turns = turns - jnp.round(turns)
            w = 0.25 - jnp.abs(turns)
            square = w * w
            poly = coefficients[-1]
            for coefficient in coefficients[-2::-1]:
                poly = poly * square + coefficient
            value = (poly * w).astype(jnp.bfloat16)
            phi[block, span] = value
            wide = value.astype(jnp.float32)
            wide = wide * wide
            for j in range(4):
                total = total + wide[:, j * LANES : (j + 1) * LANES]
        squares[experts, block, :] = total
        return carry

    lax.fori_loop(0, rows // ROWS, feature_rows, 0)

    for e in range(experts):
        for n in range(chunks):
            large[e * chunks + n].wait()
            projected = jnp.dot(
                phi[...],
                factor[e, :, n * COLUMNS : (n + 1) * COLUMNS],
                preferred_element_type=jnp.float32,
            )
            projected = projected * projected
            total = projected[:, :LANES]
            for j in range(1, COLUMNS // LANES):
                total = total + projected[:, j * LANES : (j + 1) * LANES]
            squares[e] = total if n == 0 else squares[e] + total
    small[5].wait()

    low_half = lax.broadcasted_iota(jnp.int32, (1, 8, LANES), 1) < 4
    step = 128
    for m in range(rows // step):
        block = slice(m * step, (m + 1) * step)
        prior = noise[...] + scale[...] * jnp.sum(squares[experts, block, :], axis=1, keepdims=True)
        log_prior = jnp.log(prior)
        inv_prior = 1.0 / prior
        numer = jnp.zeros((step, LANES), jnp.float32)
        denom = inv_prior * (1.0 / devices)
        for e in range(experts):
            variance = noise[...] + scale[...] * jnp.sum(squares[e, block, :], axis=1, keepdims=True)
            mean = jnp.dot(phi[block, :], means[e], preferred_element_type=jnp.float32)
            robust = jnp.maximum(0.5 * (log_prior - jnp.log(variance)), 0.0)
            inv_variance = 1.0 / variance
            numer = numer + robust * inv_variance * mean
            denom = denom + robust * (inv_variance - inv_prior)
        numer = numer.reshape(step // 8, 8, LANES)
        denom = denom.reshape(step // 8, 8, LANES)
        tiles = slice(m * step // 8, (m + 1) * step // 8)
        out_ref[tiles, 0] = jnp.where(low_half, numer, pltpu.roll(denom, 4, 1))
        out_ref[tiles, 1] = jnp.where(low_half, pltpu.roll(numer, 4, 1), denom)


def experts_sums(devices, settings, frequencies, phases, noise_var, signal_scale, cov_factor, post_mean):
    experts, feats, _ = cov_factor.shape
    rows, params = settings.shape
    comps = noise_var.shape[0]
    f32, bf16 = jnp.float32, jnp.bfloat16
    sums = pl.pallas_call(
        functools.partial(experts_kernel, devices),
        out_shape=jax.ShapeDtypeStruct((rows // 8, 2, 8, comps), f32),
        in_specs=[pl.BlockSpec(memory_space=pltpu.HBM)] * 7,
        out_specs=pl.BlockSpec(memory_space=pltpu.VMEM),
        scratch_shapes=[
            pltpu.VMEM((params, rows), f32),
            pltpu.VMEM((params, feats), f32),
            pltpu.VMEM((1, feats), f32),
            pltpu.VMEM((1, comps), f32),
            pltpu.VMEM((1, comps), f32),
            pltpu.VMEM((experts, feats, feats), bf16),
            pltpu.VMEM((experts, feats, comps), bf16),
            pltpu.VMEM((rows, feats), bf16),
            pltpu.VMEM((rows, feats), f32),
            pltpu.VMEM((experts + 1, rows, comps), f32),
            pltpu.SemaphoreType.DMA((6,)),
            pltpu.SemaphoreType.DMA((experts * (feats // COLUMNS),)),
        ],
        compiler_params=pltpu.CompilerParams(vmem_limit_bytes=60 * 2**20),
        cost_estimate=pl.CostEstimate(
            flops=2 * experts * rows * feats * (feats + comps),
            bytes_accessed=2 * experts * feats * (feats + comps),
            transcendentals=0,
        ),
    )(
        settings.T,
        frequencies,
        phases[None, :],
        noise_var[None, :],
        signal_scale[None, :],
        cov_factor,
        post_mean,
    )
    return sums.reshape(rows // 4, 8, comps)


def per_device(
    devices,
    settings,
    frequencies,
    phases,
    noise_var,
    signal_scale,
    cov_factor,
    post_mean,
    component_basis,
    mean_field,
):
    relaid = lax.all_to_all(component_basis, "ey", split_axis=1, concat_axis=0, tiled=True)
    sums = experts_sums(
        devices, settings, frequencies, phases, noise_var, signal_scale, cov_factor, post_mean
    )
    relaid, sums = lax.optimization_barrier((relaid, sums))
    parts = lax.all_to_all(sums, AXES, split_axis=0, concat_axis=0, tiled=True)
    total = jnp.sum(parts, axis=0)
    mine = (total[:4] / total[4:]).astype(jnp.bfloat16)
    copies = jnp.broadcast_to(mine[None], (devices,) + mine.shape)
    weights = lax.all_to_all(copies, AXES, split_axis=0, concat_axis=0, tiled=True)
    weights = weights.reshape(settings.shape[0], noise_var.shape[0])
    stock = jnp.dot(weights, relaid, preferred_element_type=jnp.float32) + mean_field[None, :]
    return stock.astype(jnp.bfloat16)


def solution(mesh):
    in_specs = (
        P(),
        P(),
        P(),
        P(),
        P(),
        P(AXES, None, None),
        P(AXES, None, None),
        P("ey", "ex"),
        P(AXES),
    )
    out_specs = P(None, AXES)
    return jax.shard_map(
        functools.partial(per_device, mesh.size),
        mesh=mesh,
        in_specs=in_specs,
        out_specs=out_specs,
        check_vma=False,
    )
```

```python
import functools
import math

import jax
import jax.numpy as jnp
import numpy as np
from jax import lax
from jax.experimental import pallas as pl
from jax.experimental.pallas import tpu as pltpu
from jax.sharding import Mesh
from jax.sharding import PartitionSpec as P

EX = ("y_lo", "x", "core")
EY = ("y_hi", "z")
AXES = EX + EY
PLANE = ("y_lo", "y_hi", "z")
COLUMNS = 512
ROWS = 32
LANES = 128


def sine_coefficients(terms):
    nodes = 64
    square = (1 / 16) * (0.5 + 0.5 * np.cos((2 * np.arange(nodes) + 1) * np.pi / (2 * nodes)))
    w = np.sqrt(square)
    powers = np.stack([square**i for i in range(terms)], 1) * w[:, None]
    fit, *_ = np.linalg.lstsq(powers, np.sin(2 * np.pi * w), rcond=None)
    return [float(c) for c in fit]


def split(values):
    high = values.astype(jnp.bfloat16)
    rest = values - high.astype(jnp.float32)
    middle = rest.astype(jnp.bfloat16)
    low = (rest - middle.astype(jnp.float32)).astype(jnp.bfloat16)
    return high, middle, low


def experts_kernel(
    devices,
    settings,
    frequencies,
    phases,
    noise,
    scale,
    factor_hbm,
    mean_hbm,
    keep_ref,
    send_ref,
    factor,
    means,
    phi,
    argument,
    squares,
    sums,
    sems,
):
    experts, feats, _ = factor.shape
    rows = phi.shape[0]
    chunks = feats // COLUMNS
    large = [
        pltpu.make_async_copy(
            factor_hbm.at[e, :, pl.ds(n * COLUMNS, COLUMNS)],
            factor.at[e, :, pl.ds(n * COLUMNS, COLUMNS)],
            sems.at[e * chunks + n],
        )
        for e in range(experts)
        for n in range(chunks)
    ]
    mean_copy = pltpu.make_async_copy(mean_hbm, means, sems.at[experts * chunks])
    for copy in large + [mean_copy]:
        copy.start()

    turn = 1.0 / (2.0 * math.pi)
    a0, a1, a2 = split(settings[...])
    b0, b1, b2 = split(frequencies[...] * turn)
    argument[...] = lax.dot_general(
        jnp.concatenate([a0, a0, a1, a1, a0, a2], 0),
        jnp.concatenate([b0, b1, b0, b1, b2, b0], 0),
        (((0,), (0,)), ((), ())),
        preferred_element_type=jnp.float32,
    )
    amplitude = math.sqrt(2.0 / feats)
    coefficients = [c * amplitude for c in sine_coefficients(5)]

    def feature_rows(r, carry):
        block = pl.ds(pl.multiple_of(r * ROWS, ROWS), ROWS)
        total = jnp.zeros((ROWS, LANES), jnp.float32)
        for c in range(feats // 512):
            span = slice(c * 512, (c + 1) * 512)
            turns = argument[block, span] + phases[:, span] * turn
            turns = turns - jnp.round(turns)
            w = 0.25 - jnp.abs(turns)
            square = w * w
            poly = coefficients[-1]
            for coefficient in coefficients[-2::-1]:
                poly = poly * square + coefficient
            value = (poly * w).astype(jnp.bfloat16)
            phi[block, span] = value
            wide = value.astype(jnp.float32)
            wide = wide * wide
            for j in range(4):
                total = total + wide[:, j * LANES : (j + 1) * LANES]
        squares[experts, block, :] = total
        return carry

    lax.fori_loop(0, rows // ROWS, feature_rows, 0)

    for e in range(experts):
        for n in range(chunks):
            large[e * chunks + n].wait()
            projected = jnp.dot(
                phi[...],
                factor[e, :, n * COLUMNS : (n + 1) * COLUMNS],
                preferred_element_type=jnp.float32,
            )
            projected = projected * projected
            total = projected[:, :LANES]
            for j in range(1, COLUMNS // LANES):
                total = total + projected[:, j * LANES : (j + 1) * LANES]
            squares[e] = total if n == 0 else squares[e] + total
    mean_copy.wait()

    low_half = lax.broadcasted_iota(jnp.int32, (1, 8, LANES), 1) < 4
    step = 128
    for m in range(rows // step):
        block = slice(m * step, (m + 1) * step)
        prior = noise[...] + scale[...] * jnp.sum(squares[experts, block, :], axis=1, keepdims=True)
        log_prior = jnp.log(prior)
        inv_prior = 1.0 / prior
        numer = jnp.zeros((step, LANES), jnp.float32)
        denom = inv_prior * (1.0 / devices)
        for e in range(experts):
            variance = noise[...] + scale[...] * jnp.sum(squares[e, block, :], axis=1, keepdims=True)
            mean = jnp.dot(phi[block, :], means[e], preferred_element_type=jnp.float32)
            robust = jnp.maximum(0.5 * (log_prior - jnp.log(variance)), 0.0)
            inv_variance = 1.0 / variance
            numer = numer + robust * inv_variance * mean
            denom = denom + robust * (inv_variance - inv_prior)
        numer = numer.reshape(step // 8, 8, LANES)
        denom = denom.reshape(step // 8, 8, LANES)
        tiles = slice(m * step // 8, (m + 1) * step // 8)
        sums[tiles, 0] = jnp.where(low_half, numer, pltpu.roll(denom, 4, 1))
        sums[tiles, 1] = jnp.where(low_half, pltpu.roll(numer, 4, 1), denom)

    core = lax.axis_index("core")
    for g in range(rows // 64):
        for half in range(2):
            keep_ref[g, 2 * half : 2 * half + 2] = sums[pl.ds(8 * g + 4 * core + 2 * half, 2)]
            send_ref[g, 2 * half : 2 * half + 2] = sums[pl.ds(8 * g + 4 * (1 - core) + 2 * half, 2)]


def experts_sums(devices, settings, frequencies, phases, noise_var, signal_scale, cov_factor, post_mean):
    experts, feats, _ = cov_factor.shape
    rows = settings.shape[0]
    comps = noise_var.shape[0]
    f32, bf16 = jnp.float32, jnp.bfloat16
    half = jax.ShapeDtypeStruct((rows // 64, 4, 2, 8, comps), f32)
    return pl.pallas_call(
        functools.partial(experts_kernel, devices),
        out_shape=(half, half),
        in_specs=[pl.BlockSpec(memory_space=pltpu.VMEM)] * 5 + [pl.BlockSpec(memory_space=pltpu.HBM)] * 2,
        out_specs=(pl.BlockSpec(memory_space=pltpu.VMEM),) * 2,
        scratch_shapes=[
            pltpu.VMEM((experts, feats, feats), bf16),
            pltpu.VMEM((experts, feats, comps), bf16),
            pltpu.VMEM((rows, feats), bf16),
            pltpu.VMEM((rows, feats), f32),
            pltpu.VMEM((experts + 1, rows, comps), f32),
            pltpu.VMEM((rows // 8, 2, 8, comps), f32),
            pltpu.SemaphoreType.DMA((experts * (feats // COLUMNS) + 1,)),
        ],
        compiler_params=pltpu.CompilerParams(vmem_limit_bytes=48 * 2**20),
        cost_estimate=pl.CostEstimate(
            flops=2 * experts * rows * feats * (feats + comps),
            bytes_accessed=2 * experts * feats * (feats + comps),
            transcendentals=0,
        ),
    )(
        settings.T,
        frequencies,
        phases[None, :],
        noise_var[None, :],
        signal_scale[None, :],
        cov_factor,
        post_mean,
    )


def combine_kernel(keep_ref, got_ref, *refs):
    outs, total = refs[:-1], refs[-1]
    total[...] = keep_ref[...] + got_ref[...]
    x = lax.axis_index("x")
    for mask, out_ref in enumerate(outs):
        for y in range(2):
            out_ref[y] = total[4 * y + jnp.bitwise_xor(x, mask)]


def combine(keep, got):
    part = jax.ShapeDtypeStruct((2,) + keep.shape[1:], keep.dtype)
    vmem = pl.BlockSpec(memory_space=pltpu.VMEM)
    return pl.pallas_call(
        combine_kernel,
        out_shape=(part,) * 4,
        in_specs=[vmem] * 2,
        out_specs=(vmem,) * 4,
        scratch_shapes=[pltpu.VMEM(keep.shape, keep.dtype)],
        compiler_params=pltpu.CompilerParams(vmem_limit_bytes=8 * 2**20),
    )(keep, got)


def per_device(
    devices,
    settings,
    frequencies,
    phases,
    noise_var,
    signal_scale,
    cov_factor,
    post_mean,
    component_basis,
    mean_field,
):
    relaid = lax.all_to_all(component_basis, EY, split_axis=1, concat_axis=0, tiled=True)
    keep, send = experts_sums(
        devices, settings, frequencies, phases, noise_var, signal_scale, cov_factor, post_mean
    )
    got = lax.ppermute(send, "core", [(0, 1), (1, 0)])
    mine, *sends = combine(keep, got)
    for mask, part in enumerate(sends, 1):
        mine = mine + lax.ppermute(part, "x", [(i, i ^ mask) for i in range(4)])
    mine = mine.reshape(16, 8, mine.shape[-1])
    relaid, mine = lax.optimization_barrier((relaid, mine))
    parts = lax.all_to_all(mine, PLANE, split_axis=0, concat_axis=0, tiled=True)
    total = jnp.sum(parts, axis=0)
    mine = (total[:4] / total[4:]).astype(jnp.bfloat16)
    copies = jnp.broadcast_to(mine[None], (devices,) + mine.shape)
    weights = lax.all_to_all(copies, AXES, split_axis=0, concat_axis=0, tiled=True)
    weights = weights.reshape(settings.shape[0], noise_var.shape[0])
    stock = jnp.dot(weights, relaid, preferred_element_type=jnp.float32) + mean_field[None, :]
    return stock.astype(jnp.bfloat16)


def solution(mesh):
    in_specs = (
        P(),
        P(),
        P(),
        P(),
        P(),
        P(AXES, None, None),
        P(AXES, None, None),
        P(EY, EX),
        P(AXES),
    )
    out_specs = P(None, AXES)
    fine = Mesh(np.asarray(mesh.devices).reshape(2, 4, 2, 2, 4), AXES)
    return jax.shard_map(
        functools.partial(per_device, mesh.size),
        mesh=fine,
        in_specs=in_specs,
        out_specs=out_specs,
        check_vma=False,
    )
```

```python
import functools
import math

import jax
import jax.numpy as jnp
import numpy as np
from jax import lax
from jax.experimental import pallas as pl
from jax.experimental.pallas import tpu as pltpu
from jax.sharding import Mesh
from jax.sharding import PartitionSpec as P

EX = ("y_lo", "x", "core")
EY = ("y_hi", "z")
AXES = EX + EY
PLANE = ("y_lo", "y_hi", "z")
OWNERS = ("x", "core", "z")
COLUMNS = 512
ROWS = 32
LANES = 128


def sine_coefficients(terms):
    nodes = 64
    square = (1 / 16) * (0.5 + 0.5 * np.cos((2 * np.arange(nodes) + 1) * np.pi / (2 * nodes)))
    w = np.sqrt(square)
    powers = np.stack([square**i for i in range(terms)], 1) * w[:, None]
    fit, *_ = np.linalg.lstsq(powers, np.sin(2 * np.pi * w), rcond=None)
    return [float(c) for c in fit]


def split(values):
    high = values.astype(jnp.bfloat16)
    rest = values - high.astype(jnp.float32)
    middle = rest.astype(jnp.bfloat16)
    low = (rest - middle.astype(jnp.float32)).astype(jnp.bfloat16)
    return high, middle, low


def experts_kernel(
    devices,
    settings,
    frequencies,
    phases,
    noise,
    scale,
    factor_hbm,
    mean_hbm,
    keep_ref,
    send_ref,
    factor,
    means,
    phi,
    argument,
    squares,
    sums,
    sems,
):
    experts, feats, _ = factor.shape
    rows = phi.shape[0]
    chunks = feats // COLUMNS
    large = [
        pltpu.make_async_copy(
            factor_hbm.at[e, :, pl.ds(n * COLUMNS, COLUMNS)],
            factor.at[e, :, pl.ds(n * COLUMNS, COLUMNS)],
            sems.at[e * chunks + n],
        )
        for e in range(experts)
        for n in range(chunks)
    ]
    mean_copy = pltpu.make_async_copy(mean_hbm, means, sems.at[experts * chunks])
    for copy in large + [mean_copy]:
        copy.start()

    turn = 1.0 / (2.0 * math.pi)
    a0, a1, a2 = split(settings[...])
    b0, b1, b2 = split(frequencies[...] * turn)
    argument[...] = lax.dot_general(
        jnp.concatenate([a0, a0, a1, a1, a0, a2], 0),
        jnp.concatenate([b0, b1, b0, b1, b2, b0], 0),
        (((0,), (0,)), ((), ())),
        preferred_element_type=jnp.float32,
    )
    amplitude = math.sqrt(2.0 / feats)
    coefficients = [c * amplitude for c in sine_coefficients(5)]

    def feature_rows(r, carry):
        block = pl.ds(pl.multiple_of(r * ROWS, ROWS), ROWS)
        total = jnp.zeros((ROWS, LANES), jnp.float32)
        for c in range(feats // 512):
            span = slice(c * 512, (c + 1) * 512)
            turns = argument[block, span] + phases[:, span] * turn
            turns = turns - jnp.round(turns)
            w = 0.25 - jnp.abs(turns)
            square = w * w
            poly = coefficients[-1]
            for coefficient in coefficients[-2::-1]:
                poly = poly * square + coefficient
            value = (poly * w).astype(jnp.bfloat16)
            phi[block, span] = value
            wide = value.astype(jnp.float32)
            wide = wide * wide
            for j in range(4):
                total = total + wide[:, j * LANES : (j + 1) * LANES]
        squares[experts, block, :] = total
        return carry

    lax.fori_loop(0, rows // ROWS, feature_rows, 0)

    for e in range(experts):
        for n in range(chunks):
            large[e * chunks + n].wait()
            projected = jnp.dot(
                phi[...],
                factor[e, :, n * COLUMNS : (n + 1) * COLUMNS],
                preferred_element_type=jnp.float32,
            )
            projected = projected * projected
            total = projected[:, :LANES]
            for j in range(1, COLUMNS // LANES):
                total = total + projected[:, j * LANES : (j + 1) * LANES]
            squares[e] = total if n == 0 else squares[e] + total
    mean_copy.wait()

    step = 128
    for m in range(rows // step):
        block = slice(m * step, (m + 1) * step)
        prior = noise[...] + scale[...] * jnp.sum(squares[experts, block, :], axis=1, keepdims=True)
        log_prior = jnp.log(prior)
        inv_prior = 1.0 / prior
        numer = jnp.zeros((step, LANES), jnp.float32)
        denom = inv_prior * (1.0 / devices)
        for e in range(experts):
            variance = noise[...] + scale[...] * jnp.sum(squares[e, block, :], axis=1, keepdims=True)
            mean = jnp.dot(phi[block, :], means[e], preferred_element_type=jnp.float32)
            robust = jnp.maximum(0.5 * (log_prior - jnp.log(variance)), 0.0)
            inv_variance = 1.0 / variance
            numer = numer + robust * inv_variance * mean
            denom = denom + robust * (inv_variance - inv_prior)
        sums[m] = jnp.stack([numer.reshape(-1, 16, LANES), denom.reshape(-1, 16, LANES)], axis=1)

    core = lax.axis_index("core")
    for x in range(4):
        keep_ref[x] = sums[x, pl.ds(4 * core, 4)]
        send_ref[x] = sums[x, pl.ds(4 * (1 - core), 4)]


def experts_sums(devices, settings, frequencies, phases, noise_var, signal_scale, cov_factor, post_mean):
    experts, feats, _ = cov_factor.shape
    rows = settings.shape[0]
    comps = noise_var.shape[0]
    f32, bf16 = jnp.float32, jnp.bfloat16
    half = jax.ShapeDtypeStruct((4, 4, 2, 16, comps), f32)
    return pl.pallas_call(
        functools.partial(experts_kernel, devices),
        out_shape=(half, half),
        in_specs=[pl.BlockSpec(memory_space=pltpu.VMEM)] * 5 + [pl.BlockSpec(memory_space=pltpu.HBM)] * 2,
        out_specs=(pl.BlockSpec(memory_space=pltpu.VMEM),) * 2,
        scratch_shapes=[
            pltpu.VMEM((experts, feats, feats), bf16),
            pltpu.VMEM((experts, feats, comps), bf16),
            pltpu.VMEM((rows, feats), bf16),
            pltpu.VMEM((rows, feats), f32),
            pltpu.VMEM((experts + 1, rows, comps), f32),
            pltpu.VMEM((4, 8, 2, 16, comps), f32),
            pltpu.SemaphoreType.DMA((experts * (feats // COLUMNS) + 1,)),
        ],
        compiler_params=pltpu.CompilerParams(vmem_limit_bytes=48 * 2**20),
        cost_estimate=pl.CostEstimate(
            flops=2 * experts * rows * feats * (feats + comps),
            bytes_accessed=2 * experts * feats * (feats + comps),
            transcendentals=0,
        ),
    )(
        settings.T,
        frequencies,
        phases[None, :],
        noise_var[None, :],
        signal_scale[None, :],
        cov_factor,
        post_mean,
    )


def combine_kernel(keep_ref, got_ref, *refs):
    outs, total = refs[:-1], refs[-1]
    total[...] = keep_ref[...] + got_ref[...]
    x = lax.axis_index("x")
    for mask, out_ref in enumerate(outs):
        out_ref[...] = total[jnp.bitwise_xor(x, mask)]


def combine(keep, got):
    part = jax.ShapeDtypeStruct(keep.shape[1:], keep.dtype)
    vmem = pl.BlockSpec(memory_space=pltpu.VMEM)
    return pl.pallas_call(
        combine_kernel,
        out_shape=(part,) * 4,
        in_specs=[vmem] * 2,
        out_specs=(vmem,) * 4,
        scratch_shapes=[pltpu.VMEM(keep.shape, keep.dtype)],
        compiler_params=pltpu.CompilerParams(vmem_limit_bytes=8 * 2**20),
    )(keep, got)


def relay_kernel(basis, out_ref, held, read_sems, write_sems):
    devices, _, cells = out_ref.shape
    reads = [
        pltpu.make_async_copy(basis.at[:, pl.ds(d * cells, cells)], held.at[d], read_sems.at[d])
        for d in range(devices)
    ]
    writes = [
        pltpu.make_async_copy(held.at[d], out_ref.at[d], write_sems.at[d]) for d in range(devices)
    ]
    for copy in reads:
        copy.start()
    for read, write in zip(reads, writes):
        read.wait()
        write.start()
    for copy in writes:
        copy.wait()


def relay(basis, devices):
    comps, cells = basis.shape
    shape = (devices, comps, cells // devices)
    return pl.pallas_call(
        relay_kernel,
        out_shape=jax.ShapeDtypeStruct(shape, basis.dtype),
        in_specs=[pl.BlockSpec(memory_space=pltpu.HBM)],
        out_specs=pl.BlockSpec(memory_space=pltpu.HBM),
        scratch_shapes=[
            pltpu.VMEM(shape, basis.dtype),
            pltpu.SemaphoreType.DMA((devices,)),
            pltpu.SemaphoreType.DMA((devices,)),
        ],
        compiler_params=pltpu.CompilerParams(vmem_limit_bytes=60 * 2**20),
    )(basis)


def stock_kernel(weights, basis, mean, out_ref, stock, sems):
    chunks = sems.shape[0]
    cells = basis.shape[1] // chunks
    copies = []
    for c in range(chunks):
        for n in range(cells // 256):
            span = slice(c * cells + n * 256, c * cells + (n + 1) * 256)
            tile = jnp.dot(weights[...], basis[:, span], preferred_element_type=jnp.float32)
            stock[:, span] = (tile + mean[:, span]).astype(jnp.bfloat16)
        span = pl.ds(c * cells, cells)
        copies.append(pltpu.make_async_copy(stock.at[:, span], out_ref.at[:, span], sems.at[c]))
        copies[-1].start()
    for copy in copies:
        copy.wait()


def stock_of(weights, basis, mean_field):
    rows, comps = weights.shape
    cells = mean_field.shape[0]
    chunks = 16
    vmem = pl.BlockSpec(memory_space=pltpu.VMEM)
    return pl.pallas_call(
        stock_kernel,
        out_shape=jax.ShapeDtypeStruct((rows, cells), jnp.bfloat16),
        in_specs=[vmem] * 3,
        out_specs=pl.BlockSpec(memory_space=pltpu.HBM),
        scratch_shapes=[
            pltpu.VMEM((rows, cells), jnp.bfloat16),
            pltpu.SemaphoreType.DMA((chunks,)),
        ],
        compiler_params=pltpu.CompilerParams(vmem_limit_bytes=24 * 2**20),
        cost_estimate=pl.CostEstimate(
            flops=2 * rows * comps * cells, bytes_accessed=2 * rows * cells, transcendentals=0
        ),
    )(weights, basis, mean_field[None, :])


def per_device(
    devices,
    settings,
    frequencies,
    phases,
    noise_var,
    signal_scale,
    cov_factor,
    post_mean,
    component_basis,
    mean_field,
):
    relaid = lax.all_to_all(relay(component_basis, 8), EY, split_axis=0, concat_axis=0, tiled=True)
    relaid = relaid.reshape(-1, relaid.shape[-1])
    keep, send = experts_sums(
        devices, settings, frequencies, phases, noise_var, signal_scale, cov_factor, post_mean
    )
    got = lax.ppermute(send, "core", [(0, 1), (1, 0)])
    mine, *sends = combine(keep, got)
    for mask, part in enumerate(sends, 1):
        mine = mine + lax.ppermute(part, "x", [(i, i ^ mask) for i in range(4)])
    relaid, mine = lax.optimization_barrier((relaid, mine))
    mine = jnp.broadcast_to(mine[None], (4,) + mine.shape).reshape((16,) + mine.shape[1:])
    parts = lax.all_to_all(mine, PLANE, split_axis=0, concat_axis=0, tiled=True)
    numer, denom = jnp.sum(parts, axis=0)
    mine = (numer / denom).astype(jnp.bfloat16)
    copies = jnp.broadcast_to(mine[None], (32,) + mine.shape)
    weights = lax.all_to_all(copies, OWNERS, split_axis=0, concat_axis=0, tiled=True)
    return stock_of(weights.reshape(settings.shape[0], -1), relaid, mean_field)


def solution(mesh):
    in_specs = (
        P(),
        P(),
        P(),
        P(),
        P(),
        P(AXES, None, None),
        P(AXES, None, None),
        P(EY, EX),
        P(AXES),
    )
    out_specs = P(None, AXES)
    fine = Mesh(np.asarray(mesh.devices).reshape(2, 4, 2, 2, 4), AXES)
    return jax.shard_map(
        functools.partial(per_device, mesh.size),
        mesh=fine,
        in_specs=in_specs,
        out_specs=out_specs,
        check_vma=False,
    )
```

```python
import functools
import math

import jax
import jax.numpy as jnp
import numpy as np
from jax import lax
from jax.experimental import pallas as pl
from jax.experimental.pallas import tpu as pltpu
from jax.sharding import Mesh
from jax.sharding import PartitionSpec as P

EX = ("y_lo", "x", "core")
EY = ("y_hi", "z")
AXES = EX + EY
PLANE = ("y_lo", "y_hi", "z")
OWNERS = ("x", "core", "z")
COLUMNS = 1024
ROWS = 32
LANES = 128
SHIFT = 1.5 * 2.0**23


def sine_coefficients(terms):
    nodes = 64
    square = (1 / 16) * (0.5 + 0.5 * np.cos((2 * np.arange(nodes) + 1) * np.pi / (2 * nodes)))
    w = np.sqrt(square)
    powers = np.stack([square**i for i in range(terms)], 1) * w[:, None]
    fit, *_ = np.linalg.lstsq(powers, np.sin(2 * np.pi * w), rcond=None)
    return [float(c) for c in fit]


def split(values):
    high = values.astype(jnp.bfloat16)
    rest = values - high.astype(jnp.float32)
    middle = rest.astype(jnp.bfloat16)
    low = (rest - middle.astype(jnp.float32)).astype(jnp.bfloat16)
    return high, middle, low


def experts_kernel(
    devices,
    settings,
    frequencies,
    phases,
    noise,
    scale,
    factor_hbm,
    mean_hbm,
    keep_ref,
    send_ref,
    factor,
    means,
    phi,
    argument,
    squares,
    mixed,
    sums,
    sems,
):
    experts, feats, _ = factor.shape
    rows = phi.shape[0]
    chunks = feats // COLUMNS
    large = [
        pltpu.make_async_copy(factor_hbm.at[e], factor.at[e], sems.at[e]) for e in range(experts)
    ]
    comps = noise.shape[1]
    small = [
        pltpu.make_async_copy(
            mean_hbm.at[e], means.at[:, pl.ds(e * comps, comps)], sems.at[experts + e]
        )
        for e in range(experts)
    ]
    for copy in small + large:
        copy.start()

    turn = 1.0 / (2.0 * math.pi)
    a0, a1, a2 = split(settings[...])
    b0, b1, b2 = split(frequencies[...] * turn)
    row = lax.broadcasted_iota(jnp.int32, frequencies.shape, 0)
    p0, p1, p2 = (p.astype(jnp.float32) for p in split(phases[...] * turn))
    offset = jnp.where(row == 0, p0, jnp.where(row == 1, p1, jnp.where(row == 2, p2, 0.0)))
    ones = (lax.broadcasted_iota(jnp.int32, settings.shape, 0) < 3).astype(jnp.bfloat16)
    argument[...] = lax.dot_general(
        jnp.concatenate([a0, a0, a1, a1, a0, a2, ones], 0),
        jnp.concatenate([b0, b1, b0, b1, b2, b0, offset.astype(jnp.bfloat16)], 0),
        (((0,), (0,)), ((), ())),
        preferred_element_type=jnp.float32,
    )
    amplitude = math.sqrt(2.0 / feats)
    coefficients = [c * amplitude for c in sine_coefficients(4)]

    def feature_rows(r, carry):
        block = pl.ds(pl.multiple_of(r * ROWS, ROWS), ROWS)
        total = jnp.zeros((ROWS, LANES), jnp.float32)
        for c in range(feats // 512):
            span = slice(c * 512, (c + 1) * 512)
            turns = argument[block, span]
            turns = turns - ((turns + SHIFT) - SHIFT)
            w = 0.25 - jnp.abs(turns)
            square = w * w
            poly = coefficients[-1]
            for coefficient in coefficients[-2::-1]:
                poly = poly * square + coefficient
            value = (poly * w).astype(jnp.bfloat16)
            phi[block, span] = value
            wide = value.astype(jnp.float32)
            wide = wide * wide
            for j in range(4):
                total = total + wide[:, j * LANES : (j + 1) * LANES]
        squares[experts, block, :] = total
        return carry

    lax.fori_loop(0, rows // ROWS, feature_rows, 0)

    for copy in small:
        copy.wait()
    mixed[...] = jnp.dot(phi[...], means[...], preferred_element_type=jnp.float32)
    for e in range(experts):
        large[e].wait()
        for n in range(chunks):
            projected = jnp.dot(
                phi[...],
                factor[e, :, n * COLUMNS : (n + 1) * COLUMNS],
                preferred_element_type=jnp.float32,
            )
            projected = projected * projected
            total = projected[:, :LANES]
            for j in range(1, COLUMNS // LANES):
                total = total + projected[:, j * LANES : (j + 1) * LANES]
            squares[e] = total if n == 0 else squares[e] + total

    step = 128
    for m in range(rows // step):
        block = slice(m * step, (m + 1) * step)
        prior = noise[...] + scale[...] * jnp.sum(squares[experts, block, :], axis=1, keepdims=True)
        inv_prior = 1.0 / prior
        numer = jnp.zeros((step, LANES), jnp.float32)
        denom = inv_prior * (1.0 / devices)
        for e in range(experts):
            variance = noise[...] + scale[...] * jnp.sum(squares[e, block, :], axis=1, keepdims=True)
            mean = mixed[block, e * comps : (e + 1) * comps]
            inv_variance = 1.0 / variance
            robust = jnp.maximum(0.5 * jnp.log(prior * inv_variance), 0.0)
            numer = numer + robust * inv_variance * mean
            denom = denom + robust * (inv_variance - inv_prior)
        sums[m] = jnp.stack([numer.reshape(-1, 16, LANES), denom.reshape(-1, 16, LANES)], axis=1)

    core = lax.axis_index("core")
    for x in range(4):
        keep_ref[x] = sums[x, pl.ds(4 * core, 4)]
        send_ref[x] = sums[x, pl.ds(4 * (1 - core), 4)]


def experts_sums(devices, settings, frequencies, phases, noise_var, signal_scale, cov_factor, post_mean):
    experts, feats, _ = cov_factor.shape
    rows = settings.shape[0]
    comps = noise_var.shape[0]
    f32, bf16 = jnp.float32, jnp.bfloat16
    half = jax.ShapeDtypeStruct((4, 4, 2, 16, comps), f32)
    return pl.pallas_call(
        functools.partial(experts_kernel, devices),
        out_shape=(half, half),
        in_specs=[pl.BlockSpec(memory_space=pltpu.VMEM)] * 5 + [pl.BlockSpec(memory_space=pltpu.HBM)] * 2,
        out_specs=(pl.BlockSpec(memory_space=pltpu.VMEM),) * 2,
        scratch_shapes=[
            pltpu.VMEM((experts, feats, feats), bf16),
            pltpu.VMEM((feats, experts * comps), bf16),
            pltpu.VMEM((rows, feats), bf16),
            pltpu.VMEM((rows, feats), f32),
            pltpu.VMEM((experts + 1, rows, comps), f32),
            pltpu.VMEM((rows, experts * comps), f32),
            pltpu.VMEM((4, 8, 2, 16, comps), f32),
            pltpu.SemaphoreType.DMA((2 * experts,)),
        ],
        compiler_params=pltpu.CompilerParams(vmem_limit_bytes=48 * 2**20),
        cost_estimate=pl.CostEstimate(
            flops=2 * experts * rows * feats * (feats + comps),
            bytes_accessed=2 * experts * feats * (feats + comps),
            transcendentals=0,
        ),
    )(
        settings.T,
        frequencies,
        phases[None, :],
        noise_var[None, :],
        signal_scale[None, :],
        cov_factor,
        post_mean,
    )


def combine_kernel(keep_ref, got_ref, *refs):
    outs, total = refs[:-1], refs[-1]
    total[...] = keep_ref[...] + got_ref[...]
    x = lax.axis_index("x")
    for mask, out_ref in enumerate(outs):
        out_ref[...] = total[jnp.bitwise_xor(x, mask)]


def combine(keep, got):
    part = jax.ShapeDtypeStruct(keep.shape[1:], keep.dtype)
    vmem = pl.BlockSpec(memory_space=pltpu.VMEM)
    return pl.pallas_call(
        combine_kernel,
        out_shape=(part,) * 4,
        in_specs=[vmem] * 2,
        out_specs=(vmem,) * 4,
        scratch_shapes=[pltpu.VMEM(keep.shape, keep.dtype)],
        compiler_params=pltpu.CompilerParams(vmem_limit_bytes=8 * 2**20),
    )(keep, got)


def relay_kernel(basis, out_ref, held, read_sems, write_sems):
    devices, _, cells = out_ref.shape
    reads = [
        pltpu.make_async_copy(basis.at[:, pl.ds(d * cells, cells)], held.at[d], read_sems.at[d])
        for d in range(devices)
    ]
    writes = [
        pltpu.make_async_copy(held.at[d], out_ref.at[d], write_sems.at[d]) for d in range(devices)
    ]
    for copy in reads:
        copy.start()
    for read, write in zip(reads, writes):
        read.wait()
        write.start()
    for copy in writes:
        copy.wait()


def relay(basis, devices):
    comps, cells = basis.shape
    shape = (devices, comps, cells // devices)
    return pl.pallas_call(
        relay_kernel,
        out_shape=jax.ShapeDtypeStruct(shape, basis.dtype),
        in_specs=[pl.BlockSpec(memory_space=pltpu.HBM)],
        out_specs=pl.BlockSpec(memory_space=pltpu.HBM),
        scratch_shapes=[
            pltpu.VMEM(shape, basis.dtype),
            pltpu.SemaphoreType.DMA((devices,)),
            pltpu.SemaphoreType.DMA((devices,)),
        ],
        compiler_params=pltpu.CompilerParams(vmem_limit_bytes=60 * 2**20),
    )(basis)


def stock_kernel(weights, basis, mean, out_ref, stock, sems):
    chunks = sems.shape[0]
    cells = basis.shape[1] // chunks
    copies = []
    for c in range(chunks):
        for n in range(cells // 256):
            span = slice(c * cells + n * 256, c * cells + (n + 1) * 256)
            tile = jnp.dot(weights[...], basis[:, span], preferred_element_type=jnp.float32)
            stock[:, span] = (tile + mean[:, span]).astype(jnp.bfloat16)
        span = pl.ds(c * cells, cells)
        copies.append(pltpu.make_async_copy(stock.at[:, span], out_ref.at[:, span], sems.at[c]))
        copies[-1].start()
    for copy in copies:
        copy.wait()


def stock_of(weights, basis, mean_field):
    rows, comps = weights.shape
    cells = mean_field.shape[0]
    chunks = 16
    vmem = pl.BlockSpec(memory_space=pltpu.VMEM)
    return pl.pallas_call(
        stock_kernel,
        out_shape=jax.ShapeDtypeStruct((rows, cells), jnp.bfloat16),
        in_specs=[vmem] * 3,
        out_specs=pl.BlockSpec(memory_space=pltpu.HBM),
        scratch_shapes=[
            pltpu.VMEM((rows, cells), jnp.bfloat16),
            pltpu.SemaphoreType.DMA((chunks,)),
        ],
        compiler_params=pltpu.CompilerParams(vmem_limit_bytes=24 * 2**20),
        cost_estimate=pl.CostEstimate(
            flops=2 * rows * comps * cells, bytes_accessed=2 * rows * cells, transcendentals=0
        ),
    )(weights, basis, mean_field[None, :])


def per_device(
    devices,
    settings,
    frequencies,
    phases,
    noise_var,
    signal_scale,
    cov_factor,
    post_mean,
    component_basis,
    mean_field,
):
    relaid = lax.all_to_all(relay(component_basis, 8), EY, split_axis=0, concat_axis=0, tiled=True)
    relaid = relaid.reshape(-1, relaid.shape[-1])
    keep, send = experts_sums(
        devices, settings, frequencies, phases, noise_var, signal_scale, cov_factor, post_mean
    )
    got = lax.ppermute(send, "core", [(0, 1), (1, 0)])
    mine, *sends = combine(keep, got)
    for mask, part in enumerate(sends, 1):
        mine = mine + lax.ppermute(part, "x", [(i, i ^ mask) for i in range(4)])
    relaid, mine = lax.optimization_barrier((relaid, mine))
    mine = jnp.broadcast_to(mine[None], (4,) + mine.shape).reshape((16,) + mine.shape[1:])
    parts = lax.all_to_all(mine, PLANE, split_axis=0, concat_axis=0, tiled=True)
    numer, denom = jnp.sum(parts, axis=0)
    mine = (numer / denom).astype(jnp.bfloat16)
    copies = jnp.broadcast_to(mine[None], (32,) + mine.shape)
    weights = lax.all_to_all(copies, OWNERS, split_axis=0, concat_axis=0, tiled=True)
    return stock_of(weights.reshape(settings.shape[0], -1), relaid, mean_field)


def solution(mesh):
    in_specs = (
        P(),
        P(),
        P(),
        P(),
        P(),
        P(AXES, None, None),
        P(AXES, None, None),
        P(EY, EX),
        P(AXES),
    )
    out_specs = P(None, AXES)
    fine = Mesh(np.asarray(mesh.devices).reshape(2, 4, 2, 2, 4), AXES)
    return jax.shard_map(
        functools.partial(per_device, mesh.size),
        mesh=fine,
        in_specs=in_specs,
        out_specs=out_specs,
        check_vma=False,
    )
```

```python
import functools
import math

import jax
import jax.numpy as jnp
import numpy as np
from jax import lax
from jax.experimental import pallas as pl
from jax.experimental.pallas import tpu as pltpu
from jax.sharding import Mesh
from jax.sharding import PartitionSpec as P

EX = ("y_lo", "x", "core")
EY = ("y_hi", "z_hi", "z_lo")
AXES = EX + EY
PLANE = ("y_lo", "y_hi", "z_hi", "z_lo")
OWNERS = ("x", "core", "z_lo")
COLUMNS = 1024
ROWS = 32
LANES = 128
SHIFT = 1.5 * 2.0**23


def sine_coefficients(terms):
    nodes = 64
    square = (1 / 16) * (0.5 + 0.5 * np.cos((2 * np.arange(nodes) + 1) * np.pi / (2 * nodes)))
    w = np.sqrt(square)
    powers = np.stack([square**i for i in range(terms)], 1) * w[:, None]
    fit, *_ = np.linalg.lstsq(powers, np.sin(2 * np.pi * w), rcond=None)
    return [float(c) for c in fit]


def split(values):
    high = values.astype(jnp.bfloat16)
    rest = values - high.astype(jnp.float32)
    middle = rest.astype(jnp.bfloat16)
    low = (rest - middle.astype(jnp.float32)).astype(jnp.bfloat16)
    return high, middle, low


def experts_kernel(
    devices,
    settings,
    frequencies,
    phases,
    noise,
    scale,
    factor_hbm,
    mean_hbm,
    keep_ref,
    send_ref,
    factor,
    means,
    phi,
    argument,
    squares,
    mixed,
    sums,
    sems,
):
    experts, feats, _ = factor.shape
    rows = phi.shape[0]
    chunks = feats // COLUMNS
    large = [
        pltpu.make_async_copy(factor_hbm.at[e], factor.at[e], sems.at[e]) for e in range(experts)
    ]
    comps = noise.shape[1]
    small = [
        pltpu.make_async_copy(
            mean_hbm.at[e], means.at[:, pl.ds(e * comps, comps)], sems.at[experts + e]
        )
        for e in range(experts)
    ]
    for copy in small + large:
        copy.start()

    turn = 1.0 / (2.0 * math.pi)
    a0, a1, a2 = split(settings[...])
    b0, b1, b2 = split(frequencies[...] * turn)
    row = lax.broadcasted_iota(jnp.int32, frequencies.shape, 0)
    p0, p1, p2 = (p.astype(jnp.float32) for p in split(phases[...] * turn))
    offset = jnp.where(row == 0, p0, jnp.where(row == 1, p1, jnp.where(row == 2, p2, 0.0)))
    ones = (lax.broadcasted_iota(jnp.int32, settings.shape, 0) < 3).astype(jnp.bfloat16)
    argument[...] = lax.dot_general(
        jnp.concatenate([a0, a0, a1, a1, a0, a2, ones], 0),
        jnp.concatenate([b0, b1, b0, b1, b2, b0, offset.astype(jnp.bfloat16)], 0),
        (((0,), (0,)), ((), ())),
        preferred_element_type=jnp.float32,
    )
    amplitude = math.sqrt(2.0 / feats)
    coefficients = [c * amplitude for c in sine_coefficients(5)]

    def feature_rows(r, carry):
        block = pl.ds(pl.multiple_of(r * ROWS, ROWS), ROWS)
        total = jnp.zeros((ROWS, LANES), jnp.float32)
        for c in range(feats // 512):
            span = slice(c * 512, (c + 1) * 512)
            turns = argument[block, span]
            turns = turns - ((turns + SHIFT) - SHIFT)
            w = 0.25 - jnp.abs(turns)
            square = w * w
            poly = coefficients[-1]
            for coefficient in coefficients[-2::-1]:
                poly = poly * square + coefficient
            value = (poly * w).astype(jnp.bfloat16)
            phi[block, span] = value
            wide = value.astype(jnp.float32)
            wide = wide * wide
            for j in range(4):
                total = total + wide[:, j * LANES : (j + 1) * LANES]
        squares[experts, block, :] = total
        return carry

    lax.fori_loop(0, rows // ROWS, feature_rows, 0)

    for copy in small:
        copy.wait()
    mixed[...] = jnp.dot(phi[...], means[...], preferred_element_type=jnp.float32)
    for e in range(experts):
        large[e].wait()
        for n in range(chunks):
            projected = jnp.dot(
                phi[...],
                factor[e, :, n * COLUMNS : (n + 1) * COLUMNS],
                preferred_element_type=jnp.float32,
            )
            projected = projected * projected
            total = projected[:, :LANES]
            for j in range(1, COLUMNS // LANES):
                total = total + projected[:, j * LANES : (j + 1) * LANES]
            squares[e] = total if n == 0 else squares[e] + total

    step = 128
    for m in range(rows // step):
        block = slice(m * step, (m + 1) * step)
        prior = noise[...] + scale[...] * jnp.sum(squares[experts, block, :], axis=1, keepdims=True)
        inv_prior = 1.0 / prior
        numer = jnp.zeros((step, LANES), jnp.float32)
        denom = inv_prior * (1.0 / devices)
        for e in range(experts):
            variance = noise[...] + scale[...] * jnp.sum(squares[e, block, :], axis=1, keepdims=True)
            mean = mixed[block, e * comps : (e + 1) * comps]
            inv_variance = 1.0 / variance
            robust = jnp.maximum(0.5 * jnp.log(prior * inv_variance), 0.0)
            numer = numer + robust * inv_variance * mean
            denom = denom + robust * (inv_variance - inv_prior)
        sums[m] = jnp.stack([numer.reshape(-1, 32, LANES), denom.reshape(-1, 32, LANES)], axis=1)

    core = lax.axis_index("core")
    for x in range(4):
        keep_ref[x] = sums[x, pl.ds(2 * core, 2)]
        send_ref[x] = sums[x, pl.ds(2 * (1 - core), 2)]


def experts_sums(devices, settings, frequencies, phases, noise_var, signal_scale, cov_factor, post_mean):
    experts, feats, _ = cov_factor.shape
    rows = settings.shape[0]
    comps = noise_var.shape[0]
    f32, bf16 = jnp.float32, jnp.bfloat16
    half = jax.ShapeDtypeStruct((4, 2, 2, 32, comps), f32)
    return pl.pallas_call(
        functools.partial(experts_kernel, devices),
        out_shape=(half, half),
        in_specs=[pl.BlockSpec(memory_space=pltpu.VMEM)] * 5 + [pl.BlockSpec(memory_space=pltpu.HBM)] * 2,
        out_specs=(pl.BlockSpec(memory_space=pltpu.VMEM),) * 2,
        scratch_shapes=[
            pltpu.VMEM((experts, feats, feats), bf16),
            pltpu.VMEM((feats, experts * comps), bf16),
            pltpu.VMEM((rows, feats), bf16),
            pltpu.VMEM((rows, feats), f32),
            pltpu.VMEM((experts + 1, rows, comps), f32),
            pltpu.VMEM((rows, experts * comps), f32),
            pltpu.VMEM((4, 4, 2, 32, comps), f32),
            pltpu.SemaphoreType.DMA((2 * experts,)),
        ],
        compiler_params=pltpu.CompilerParams(vmem_limit_bytes=48 * 2**20),
        cost_estimate=pl.CostEstimate(
            flops=2 * experts * rows * feats * (feats + comps),
            bytes_accessed=2 * experts * feats * (feats + comps),
            transcendentals=0,
        ),
    )(
        settings.T,
        frequencies,
        phases[None, :],
        noise_var[None, :],
        signal_scale[None, :],
        cov_factor,
        post_mean,
    )


def combine_kernel(keep_ref, got_ref, *refs):
    outs, total = refs[:-1], refs[-1]
    total[...] = keep_ref[...] + got_ref[...]
    x = lax.axis_index("x")
    for mask, out_ref in enumerate(outs):
        out_ref[...] = total[jnp.bitwise_xor(x, mask)]


def combine(keep, got):
    part = jax.ShapeDtypeStruct(keep.shape[1:], keep.dtype)
    vmem = pl.BlockSpec(memory_space=pltpu.VMEM)
    return pl.pallas_call(
        combine_kernel,
        out_shape=(part,) * 4,
        in_specs=[vmem] * 2,
        out_specs=(vmem,) * 4,
        scratch_shapes=[pltpu.VMEM(keep.shape, keep.dtype)],
        compiler_params=pltpu.CompilerParams(vmem_limit_bytes=8 * 2**20),
    )(keep, got)


def pack_kernel(*refs):
    parts, out_ref = refs[:-1], refs[-1]
    groups = parts[0].shape[0]
    for g in range(groups):
        numer, denom = (
            (parts[0][g, k] + parts[1][g, k]) + (parts[2][g, k] + parts[3][g, k]) for k in range(2)
        )
        high = numer.astype(jnp.bfloat16)
        low = (numer - high.astype(jnp.float32)).astype(jnp.bfloat16)
        denom = denom.astype(jnp.bfloat16)
        for copy in range(out_ref.shape[0] // groups):
            out_ref[copy * groups + g, 0] = high
            out_ref[copy * groups + g, 1] = low
            out_ref[copy * groups + g, 2] = denom


def pack(parts, devices):
    _, _, depth, comps = parts[0].shape
    vmem = pl.BlockSpec(memory_space=pltpu.VMEM)
    return pl.pallas_call(
        pack_kernel,
        out_shape=jax.ShapeDtypeStruct((devices, 3, depth, comps), jnp.bfloat16),
        in_specs=[vmem] * len(parts),
        out_specs=vmem,
        compiler_params=pltpu.CompilerParams(vmem_limit_bytes=8 * 2**20),
    )(*parts)


def relay_kernel(basis, out_ref, held, read_sems, write_sems):
    devices, _, cells = out_ref.shape
    reads = [
        pltpu.make_async_copy(basis.at[:, pl.ds(d * cells, cells)], held.at[d], read_sems.at[d])
        for d in range(devices)
    ]
    writes = [
        pltpu.make_async_copy(held.at[d], out_ref.at[d], write_sems.at[d]) for d in range(devices)
    ]
    for copy in reads:
        copy.start()
    for read, write in zip(reads, writes):
        read.wait()
        write.start()
    for copy in writes:
        copy.wait()


def relay(basis, devices):
    comps, cells = basis.shape
    shape = (devices, comps, cells // devices)
    return pl.pallas_call(
        relay_kernel,
        out_shape=jax.ShapeDtypeStruct(shape, basis.dtype),
        in_specs=[pl.BlockSpec(memory_space=pltpu.HBM)],
        out_specs=pl.BlockSpec(memory_space=pltpu.HBM),
        scratch_shapes=[
            pltpu.VMEM(shape, basis.dtype),
            pltpu.SemaphoreType.DMA((devices,)),
            pltpu.SemaphoreType.DMA((devices,)),
        ],
        compiler_params=pltpu.CompilerParams(vmem_limit_bytes=60 * 2**20),
    )(basis)


def stock_kernel(weights, basis, mean, out_ref, stock, sems):
    chunks = sems.shape[0]
    cells = basis.shape[1] // chunks
    copies = []
    for c in range(chunks):
        for n in range(cells // 256):
            span = slice(c * cells + n * 256, c * cells + (n + 1) * 256)
            tile = jnp.dot(weights[...], basis[:, span], preferred_element_type=jnp.float32)
            stock[:, span] = (tile + mean[:, span]).astype(jnp.bfloat16)
        span = pl.ds(c * cells, cells)
        copies.append(pltpu.make_async_copy(stock.at[:, span], out_ref.at[:, span], sems.at[c]))
        copies[-1].start()
    for copy in copies:
        copy.wait()


def stock_of(weights, basis, mean_field):
    rows, comps = weights.shape
    cells = mean_field.shape[0]
    chunks = 16
    vmem = pl.BlockSpec(memory_space=pltpu.VMEM)
    return pl.pallas_call(
        stock_kernel,
        out_shape=jax.ShapeDtypeStruct((rows, cells), jnp.bfloat16),
        in_specs=[vmem] * 3,
        out_specs=pl.BlockSpec(memory_space=pltpu.HBM),
        scratch_shapes=[
            pltpu.VMEM((rows, cells), jnp.bfloat16),
            pltpu.SemaphoreType.DMA((chunks,)),
        ],
        compiler_params=pltpu.CompilerParams(vmem_limit_bytes=24 * 2**20),
        cost_estimate=pl.CostEstimate(
            flops=2 * rows * comps * cells, bytes_accessed=2 * rows * cells, transcendentals=0
        ),
    )(weights, basis, mean_field[None, :])


def per_device(
    devices,
    settings,
    frequencies,
    phases,
    noise_var,
    signal_scale,
    cov_factor,
    post_mean,
    component_basis,
    mean_field,
):
    relaid = lax.all_to_all(relay(component_basis, 8), EY, split_axis=0, concat_axis=0, tiled=True)
    relaid = relaid.reshape(-1, relaid.shape[-1])
    keep, send = experts_sums(
        devices, settings, frequencies, phases, noise_var, signal_scale, cov_factor, post_mean
    )
    got = lax.ppermute(send, "core", [(0, 1), (1, 0)])
    mine, *sends = combine(keep, got)
    parts = [mine] + [
        lax.ppermute(part, "x", [(i, i ^ mask) for i in range(4)])
        for mask, part in enumerate(sends, 1)
    ]
    packed = pack(parts, 16)
    relaid, packed = lax.optimization_barrier((relaid, packed))
    got = lax.all_to_all(packed, PLANE, split_axis=0, concat_axis=0, tiled=True)
    high, low, denom = jnp.sum(got.astype(jnp.float32), axis=0)
    numer = high + low
    mine = (numer / denom).astype(jnp.bfloat16)
    copies = jnp.broadcast_to(mine[None], (16,) + mine.shape)
    weights = lax.all_to_all(copies, OWNERS, split_axis=0, concat_axis=0, tiled=True)
    return stock_of(weights.reshape(settings.shape[0], -1), relaid, mean_field)


def solution(mesh):
    in_specs = (
        P(),
        P(),
        P(),
        P(),
        P(),
        P(AXES, None, None),
        P(AXES, None, None),
        P(EY, EX),
        P(AXES),
    )
    out_specs = P(None, AXES)
    fine = Mesh(np.asarray(mesh.devices).reshape(2, 4, 2, 2, 2, 2), AXES)
    return jax.shard_map(
        functools.partial(per_device, mesh.size),
        mesh=fine,
        in_specs=in_specs,
        out_specs=out_specs,
        check_vma=False,
    )
```

```python
import functools
import math

import jax
import jax.numpy as jnp
import numpy as np
from jax import lax
from jax.experimental import pallas as pl
from jax.experimental.pallas import tpu as pltpu
from jax.sharding import Mesh
from jax.sharding import PartitionSpec as P

EX = ("y_lo", "x", "core")
EY = ("y_hi", "z_hi", "z_lo")
AXES = EX + EY
PLANE = ("y_lo", "y_hi", "z_hi", "z_lo")
OWNERS = ("x", "core", "z_lo")
COLUMNS = 1024
ROWS = 32
LANES = 128
SHIFT = 1.5 * 2.0**23


def sine_coefficients(terms):
    nodes = 64
    square = (1 / 16) * (0.5 + 0.5 * np.cos((2 * np.arange(nodes) + 1) * np.pi / (2 * nodes)))
    w = np.sqrt(square)
    powers = np.stack([square**i for i in range(terms)], 1) * w[:, None]
    fit, *_ = np.linalg.lstsq(powers, np.sin(2 * np.pi * w), rcond=None)
    return [float(c) for c in fit]


def split(values):
    high = values.astype(jnp.bfloat16)
    rest = values - high.astype(jnp.float32)
    middle = rest.astype(jnp.bfloat16)
    low = (rest - middle.astype(jnp.float32)).astype(jnp.bfloat16)
    return high, middle, low


def experts_kernel(
    devices,
    settings,
    frequencies,
    phases,
    noise,
    scale,
    factor_hbm,
    mean_hbm,
    keep_ref,
    send_ref,
    factor,
    means,
    phi,
    argument,
    squares,
    mixed,
    sums,
    sems,
):
    experts, feats, _ = factor.shape
    rows = phi.shape[0]
    chunks = feats // COLUMNS
    large = [
        pltpu.make_async_copy(factor_hbm.at[e], factor.at[e], sems.at[e]) for e in range(experts)
    ]
    comps = noise.shape[1]
    small = [
        pltpu.make_async_copy(
            mean_hbm.at[e], means.at[:, pl.ds(e * comps, comps)], sems.at[experts + e]
        )
        for e in range(experts)
    ]
    for copy in small + large:
        copy.start()

    turn = 1.0 / (2.0 * math.pi)
    a0, a1, a2 = split(settings[...])
    b0, b1, b2 = split(frequencies[...] * turn)
    row = lax.broadcasted_iota(jnp.int32, frequencies.shape, 0)
    p0, p1, p2 = (p.astype(jnp.float32) for p in split(phases[...] * turn))
    offset = jnp.where(row == 0, p0, jnp.where(row == 1, p1, jnp.where(row == 2, p2, 0.0)))
    ones = (lax.broadcasted_iota(jnp.int32, settings.shape, 0) < 3).astype(jnp.bfloat16)
    argument[...] = lax.dot_general(
        jnp.concatenate([a0, a0, a1, a1, a0, a2, ones], 0),
        jnp.concatenate([b0, b1, b0, b1, b2, b0, offset.astype(jnp.bfloat16)], 0),
        (((0,), (0,)), ((), ())),
        preferred_element_type=jnp.float32,
    )
    amplitude = math.sqrt(2.0 / feats)
    coefficients = [c * amplitude for c in sine_coefficients(4)]

    def feature_rows(r, carry):
        block = pl.ds(pl.multiple_of(r * ROWS, ROWS), ROWS)
        total = jnp.zeros((ROWS, LANES), jnp.float32)
        for c in range(feats // 512):
            span = slice(c * 512, (c + 1) * 512)
            turns = argument[block, span]
            turns = turns - ((turns + SHIFT) - SHIFT)
            w = 0.25 - jnp.abs(turns)
            square = w * w
            poly = coefficients[-1]
            for coefficient in coefficients[-2::-1]:
                poly = poly * square + coefficient
            value = (poly * w).astype(jnp.bfloat16)
            phi[block, span] = value
            wide = value.astype(jnp.float32)
            wide = wide * wide
            for j in range(4):
                total = total + wide[:, j * LANES : (j + 1) * LANES]
        squares[experts, block, :] = total
        return carry

    lax.fori_loop(0, rows // ROWS, feature_rows, 0)

    for copy in small:
        copy.wait()
    mixed[...] = jnp.dot(phi[...], means[...], preferred_element_type=jnp.float32)
    for e in range(experts):
        large[e].wait()
        for n in range(chunks):
            projected = jnp.dot(
                phi[...],
                factor[e, :, n * COLUMNS : (n + 1) * COLUMNS],
                preferred_element_type=jnp.float32,
            )
            projected = projected * projected
            total = projected[:, :LANES]
            for j in range(1, COLUMNS // LANES):
                total = total + projected[:, j * LANES : (j + 1) * LANES]
            squares[e] = total if n == 0 else squares[e] + total

    step = 128
    for m in range(rows // step):
        block = slice(m * step, (m + 1) * step)
        prior = noise[...] + scale[...] * jnp.sum(squares[experts, block, :], axis=1, keepdims=True)
        inv_prior = 1.0 / prior
        numer = jnp.zeros((step, LANES), jnp.float32)
        denom = inv_prior * (1.0 / devices)
        for e in range(experts):
            variance = noise[...] + scale[...] * jnp.sum(squares[e, block, :], axis=1, keepdims=True)
            mean = mixed[block, e * comps : (e + 1) * comps]
            inv_variance = 1.0 / variance
            robust = jnp.maximum(0.5 * jnp.log(prior * inv_variance), 0.0)
            numer = numer + robust * inv_variance * mean
            denom = denom + robust * (inv_variance - inv_prior)
        sums[m] = jnp.stack([numer.reshape(-1, 32, LANES), denom.reshape(-1, 32, LANES)], axis=1)

    core = lax.axis_index("core")
    for x in range(4):
        keep_ref[x] = sums[x, pl.ds(2 * core, 2)]
        send_ref[x] = sums[x, pl.ds(2 * (1 - core), 2)]


def experts_sums(devices, settings, frequencies, phases, noise_var, signal_scale, cov_factor, post_mean):
    experts, feats, _ = cov_factor.shape
    rows = settings.shape[0]
    comps = noise_var.shape[0]
    f32, bf16 = jnp.float32, jnp.bfloat16
    half = jax.ShapeDtypeStruct((4, 2, 2, 32, comps), f32)
    return pl.pallas_call(
        functools.partial(experts_kernel, devices),
        out_shape=(half, half),
        in_specs=[pl.BlockSpec(memory_space=pltpu.VMEM)] * 5 + [pl.BlockSpec(memory_space=pltpu.HBM)] * 2,
        out_specs=(pl.BlockSpec(memory_space=pltpu.VMEM),) * 2,
        scratch_shapes=[
            pltpu.VMEM((experts, feats, feats), bf16),
            pltpu.VMEM((feats, experts * comps), bf16),
            pltpu.VMEM((rows, feats), bf16),
            pltpu.VMEM((rows, feats), f32),
            pltpu.VMEM((experts + 1, rows, comps), f32),
            pltpu.VMEM((rows, experts * comps), f32),
            pltpu.VMEM((4, 4, 2, 32, comps), f32),
            pltpu.SemaphoreType.DMA((2 * experts,)),
        ],
        compiler_params=pltpu.CompilerParams(vmem_limit_bytes=48 * 2**20),
        cost_estimate=pl.CostEstimate(
            flops=2 * experts * rows * feats * (feats + comps),
            bytes_accessed=2 * experts * feats * (feats + comps),
            transcendentals=0,
        ),
    )(
        settings.T,
        frequencies,
        phases[None, :],
        noise_var[None, :],
        signal_scale[None, :],
        cov_factor,
        post_mean,
    )


def combine_kernel(keep_ref, got_ref, *refs):
    outs, total = refs[:-1], refs[-1]
    total[...] = keep_ref[...] + got_ref[...]
    x = lax.axis_index("x")
    for mask, out_ref in enumerate(outs):
        out_ref[...] = total[jnp.bitwise_xor(x, mask)]


def combine(keep, got):
    part = jax.ShapeDtypeStruct(keep.shape[1:], keep.dtype)
    vmem = pl.BlockSpec(memory_space=pltpu.VMEM)
    return pl.pallas_call(
        combine_kernel,
        out_shape=(part,) * 4,
        in_specs=[vmem] * 2,
        out_specs=(vmem,) * 4,
        scratch_shapes=[pltpu.VMEM(keep.shape, keep.dtype)],
        compiler_params=pltpu.CompilerParams(vmem_limit_bytes=8 * 2**20),
    )(keep, got)


def pack_kernel(*refs):
    parts, out_ref = refs[:-1], refs[-1]
    groups = parts[0].shape[0]
    for g in range(groups):
        numer, denom = (
            (parts[0][g, k] + parts[1][g, k]) + (parts[2][g, k] + parts[3][g, k]) for k in range(2)
        )
        high = numer.astype(jnp.bfloat16)
        low = (numer - high.astype(jnp.float32)).astype(jnp.bfloat16)
        denom = denom.astype(jnp.bfloat16)
        for copy in range(out_ref.shape[0] // groups):
            out_ref[copy * groups + g, 0] = high
            out_ref[copy * groups + g, 1] = low
            out_ref[copy * groups + g, 2] = denom


def pack(parts, devices):
    _, _, depth, comps = parts[0].shape
    vmem = pl.BlockSpec(memory_space=pltpu.VMEM)
    return pl.pallas_call(
        pack_kernel,
        out_shape=jax.ShapeDtypeStruct((devices, 3, depth, comps), jnp.bfloat16),
        in_specs=[vmem] * len(parts),
        out_specs=vmem,
        compiler_params=pltpu.CompilerParams(vmem_limit_bytes=8 * 2**20),
    )(*parts)


def relay_kernel(basis, out_ref, held, read_sems, write_sems):
    devices, _, cells = out_ref.shape
    reads = [
        pltpu.make_async_copy(basis.at[:, pl.ds(d * cells, cells)], held.at[d], read_sems.at[d])
        for d in range(devices)
    ]
    writes = [
        pltpu.make_async_copy(held.at[d], out_ref.at[d], write_sems.at[d]) for d in range(devices)
    ]
    for copy in reads:
        copy.start()
    for read, write in zip(reads, writes):
        read.wait()
        write.start()
    for copy in writes:
        copy.wait()


def relay(basis, devices):
    comps, cells = basis.shape
    shape = (devices, comps, cells // devices)
    return pl.pallas_call(
        relay_kernel,
        out_shape=jax.ShapeDtypeStruct(shape, basis.dtype),
        in_specs=[pl.BlockSpec(memory_space=pltpu.HBM)],
        out_specs=pl.BlockSpec(memory_space=pltpu.HBM),
        scratch_shapes=[
            pltpu.VMEM(shape, basis.dtype),
            pltpu.SemaphoreType.DMA((devices,)),
            pltpu.SemaphoreType.DMA((devices,)),
        ],
        compiler_params=pltpu.CompilerParams(vmem_limit_bytes=60 * 2**20),
    )(basis)


def stock_kernel(weights, basis, mean, out_ref, stock, sems):
    chunks = sems.shape[0]
    cells = basis.shape[1] // chunks
    copies = []
    for c in range(chunks):
        for n in range(cells // 256):
            span = slice(c * cells + n * 256, c * cells + (n + 1) * 256)
            tile = jnp.dot(weights[...], basis[:, span], preferred_element_type=jnp.float32)
            stock[:, span] = (tile + mean[:, span]).astype(jnp.bfloat16)
        span = pl.ds(c * cells, cells)
        copies.append(pltpu.make_async_copy(stock.at[:, span], out_ref.at[:, span], sems.at[c]))
        copies[-1].start()
    for copy in copies:
        copy.wait()


def stock_of(weights, basis, mean_field):
    rows, comps = weights.shape
    cells = mean_field.shape[0]
    chunks = 16
    vmem = pl.BlockSpec(memory_space=pltpu.VMEM)
    return pl.pallas_call(
        stock_kernel,
        out_shape=jax.ShapeDtypeStruct((rows, cells), jnp.bfloat16),
        in_specs=[vmem] * 3,
        out_specs=pl.BlockSpec(memory_space=pltpu.HBM),
        scratch_shapes=[
            pltpu.VMEM((rows, cells), jnp.bfloat16),
            pltpu.SemaphoreType.DMA((chunks,)),
        ],
        compiler_params=pltpu.CompilerParams(vmem_limit_bytes=24 * 2**20),
        cost_estimate=pl.CostEstimate(
            flops=2 * rows * comps * cells, bytes_accessed=2 * rows * cells, transcendentals=0
        ),
    )(weights, basis, mean_field[None, :])


def per_device(
    devices,
    settings,
    frequencies,
    phases,
    noise_var,
    signal_scale,
    cov_factor,
    post_mean,
    component_basis,
    mean_field,
):
    relaid = lax.all_to_all(relay(component_basis, 8), EY, split_axis=0, concat_axis=0, tiled=True)
    relaid = relaid.reshape(-1, relaid.shape[-1])
    keep, send = experts_sums(
        devices, settings, frequencies, phases, noise_var, signal_scale, cov_factor, post_mean
    )
    got = lax.ppermute(send, "core", [(0, 1), (1, 0)])
    mine, *sends = combine(keep, got)
    parts = [mine] + [
        lax.ppermute(part, "x", [(i, i ^ mask) for i in range(4)])
        for mask, part in enumerate(sends, 1)
    ]
    packed = pack(parts, 16)
    relaid, packed = lax.optimization_barrier((relaid, packed))
    got = lax.all_to_all(packed, PLANE, split_axis=0, concat_axis=0, tiled=True)
    high, low, denom = jnp.sum(got.astype(jnp.float32), axis=0)
    numer = high + low
    mine = (numer / denom).astype(jnp.bfloat16)
    copies = jnp.broadcast_to(mine[None], (16,) + mine.shape)
    weights = lax.all_to_all(copies, OWNERS, split_axis=0, concat_axis=0, tiled=True)
    return stock_of(weights.reshape(settings.shape[0], -1), relaid, mean_field)


def solution(mesh):
    in_specs = (
        P(),
        P(),
        P(),
        P(),
        P(),
        P(AXES, None, None),
        P(AXES, None, None),
        P(EY, EX),
        P(AXES),
    )
    out_specs = P(None, AXES)
    fine = Mesh(np.asarray(mesh.devices).reshape(2, 4, 2, 2, 2, 2), AXES)
    return jax.shard_map(
        functools.partial(per_device, mesh.size),
        mesh=fine,
        in_specs=in_specs,
        out_specs=out_specs,
        check_vma=False,
    )
```
